32 devices in a mesh: dp: 4 (over z), expert: 8 (over y, x, core).
Axes of the slice: x: 2, y: 2, z: 4, core: 2. Of those that a mesh axis runs over, the one named last changes fastest.
Arguments:
- tokens_in: bfloat16 [4096, 4096], P(('dp', 'expert')), may hold values from -6 to 6
- out_grad: bfloat16 [4096, 4096], P(('dp', 'expert')), may hold values from -3 to 3
- expert_ids: int32 [4096, 2], P(('dp', 'expert')), may hold values from 0 to 7, all different within a row; in each aligned block of 128 rows (0 to 127, 128 to 255, ...) at most 64 rows name the same one
- gate_probs: bfloat16 [4096, 2], P(('dp', 'expert')), may hold values from 0.099609375 to 1
- gate_up: bfloat16 [4096, 2, 8, 768], P(None, None, 'expert'), may hold values from -0.09375 to 0.09375
- down_proj: bfloat16 [4096, 8, 768], P(None, 'expert'), may hold values from -0.21875 to 0.21875
Outputs:
- input_grad: bfloat16 [4096, 4096], P(('dp', 'expert'))
- gate_grad: bfloat16 [4096, 2], P(('dp', 'expert'))
- gate_up_grad: bfloat16 [4096, 2, 8, 768], P('dp', None, 'expert')
- down_grad: bfloat16 [4096, 8, 768], P('dp', 'expert')
The draws below stay inside these ranges and needn't reach their ends.
Inputs may be any that keep to these rules, and one draw needn't show every extreme that they name: `expert_ids`: each row names 2 different experts. The rows of one device name no expert more than 64 times, and in every draw some device's rows name some expert exactly 64 times.
All inputs are finite; a program needn't handle non-finite values.
Results may differ from the reference program's by a relative error of at most 0.017.
Values may be sent and summed in bfloat16 or wider, within the bound.
A program may use at most 192 MiB of HBM per device.

```python
import math
import jax
import jax.numpy as jnp
import numpy as np
from jax import lax

D = 4096
FF = 768
TOP_WIN = 2
TOK_DEV = 128
EXPERTS = 8
CAP = 64
TOKENS = 4096
N_DP = 4
N_EXPERT = 8


def shard_levels(stream_key, extent, pieces, low, largest):
    def one(dim, blocks):
        heights = jax.random.uniform(jax.random.fold_in(jax.random.fold_in(stream_key, 6), dim), (blocks,), jnp.float32, low / len(pieces), largest / len(pieces))
        return jnp.repeat(jnp.exp(heights), extent[dim] // blocks).reshape((-1,) + (1,) * (len(extent) - dim - 1))

    loudness = one(*pieces[0])
    for cut in pieces[1:]:
        loudness = loudness * one(*cut)
    return loudness


def routed_block(stream_key, own, number, rows, amount, top, most, slope):
    ranking = jax.random.permutation(stream_key, amount)
    crowded, common = shares(amount, rows * top, most, slope, True), shares(amount, rows * top, most, slope, False)
    places = jnp.arange(amount)

    def named(tallies, offset_by):
        used = int((tallies > 0).sum())
        fixed = max(1, used // 4)
        moved = fixed + (places - fixed + offset_by * (used - fixed)) % max(1, amount - fixed)
        return jnp.zeros((amount,), jnp.int32).at[ranking[jnp.where(places < fixed, places, moved)]].set(jnp.asarray(tallies, jnp.int32))

    tallies = jnp.where(number % 4 == 0, named(crowded, number // 4), named(common, number - number // 4 - 1))
    mixed = jax.random.permutation(jax.random.fold_in(own, 3), amount)
    giver, sink = mixed[0:amount // 2 * 2:2], mixed[1:amount // 2 * 2:2]
    margin = jnp.minimum(tallies[giver] - 1, most - tallies[sink]) // 2
    margin = jnp.where((giver == ranking[0]) | (sink == ranking[0]) | (tallies[sink] == 0), 0, jnp.maximum(margin, 0))
    moved = jax.random.randint(jax.random.fold_in(own, 4), (amount // 2,), 0, 1 << 20) % (margin + 1)
    tallies = tallies.at[giver].add(-moved).at[sink].add(moved)
    items = jnp.searchsorted(jnp.cumsum(tallies), jnp.arange(rows * top), side="right").astype(jnp.int32)
    grid = items.reshape(top, rows).T
    grid = grid[jax.random.permutation(jax.random.fold_in(own, 1), rows)]
    offset_by = jax.random.randint(jax.random.fold_in(own, 2), (rows, 1), 0, top)
    return jnp.take_along_axis(grid, (jnp.arange(top)[None, :] + offset_by) % top, axis=1)


def shares(number_of, total, reach, slope, full):
    loads = [(1 << 20) // math.isqrt(rank ** slope) + 1 for rank in range(1, number_of + 1)]
    largest = reach if full else min(reach, max(-(-total // number_of), total * loads[0] // sum(loads)))
    least = 1 if total - largest >= number_of - 1 else 0
    counts, surplus = [largest] + [least] * (number_of - 1), total - largest - least * (number_of - 1)
    while surplus > 0:
        candidates = [i for i in range(1, number_of) if counts[i] < largest] or [i for i in range(1, number_of) if counts[i] < reach]
        whole, budget = sum([loads[i] for i in candidates]), surplus
        for i in candidates:
            addition = min(reach - counts[i], max(1, budget * loads[i] // whole), surplus)
            counts[i] = counts[i] + addition
            surplus = surplus - addition
    return np.array(counts)


def scatter_about(rng, shape, scale, bound, split=(), kind=jnp.bfloat16):
    gain = shard_levels(rng, shape, split, -0.22, 0.18) if split else 1.0
    values = jax.random.normal(rng, shape, jnp.float32) * scale * gain
    return jnp.minimum(jnp.maximum(values, -bound), bound).astype(kind)


def setup_inputs(seed: int = 0) -> dict:
    keys = jax.random.split(jax.random.key(seed), 7)
    tokens_in = scatter_about(keys[0], (TOKENS, D), 1.0, 6.0, ((0, 32),))
    out_grad = scatter_about(keys[1], (TOKENS, D), 0.5, 3.0, ((0, 32),))
    expert_ids_keys = jax.random.split(jax.random.fold_in(keys[2], 1), TOKENS // TOK_DEV)
    expert_ids_turns = jax.random.permutation(jax.random.fold_in(keys[2], 3), TOKENS // TOK_DEV)
    expert_ids = jax.vmap(lambda own, number: routed_block(jax.random.fold_in(keys[2], 2), own, number, TOK_DEV, EXPERTS, TOP_WIN, CAP, 2))(expert_ids_keys, expert_ids_turns).reshape((TOKENS, TOP_WIN))
    gate_probs = jnp.clip(0.099609375 + 0.9003906 * jax.random.uniform(keys[3], (TOKENS, TOP_WIN), jnp.float32) ** shard_levels(keys[3], (TOKENS, TOP_WIN), ((0, 32),), -0.2, 0.2), 0.099609375, 1.0).astype(jnp.bfloat16)
    gate_up = scatter_about(keys[4], (D, 2, EXPERTS, FF), D ** -0.5, 0.09375, ((2, 8),))
    down_proj = scatter_about(keys[5], (D, EXPERTS, FF), FF ** -0.5, 0.21875, ((1, 8),))
    return {"tokens_in": tokens_in, "out_grad": out_grad, "expert_ids": expert_ids, "gate_probs": gate_probs, "gate_up": gate_up, "down_proj": down_proj}


def expert_rows(rows_in, grads_in, gates_in, gate_w, up_w, down_w):
    pre_gate = jnp.dot(rows_in, gate_w, preferred_element_type=jnp.float32)
    pre_up = jnp.dot(rows_in, up_w, preferred_element_type=jnp.float32)
    sigmoid_gate = jax.nn.sigmoid(pre_gate)
    activated = pre_gate * sigmoid_gate
    product = (activated * pre_up).astype(jnp.bfloat16)
    output_rows = jnp.dot(product, down_w.T, preferred_element_type=jnp.float32)
    gate_rows = jnp.sum(grads_in.astype(jnp.float32) * output_rows, axis=-1).astype(jnp.bfloat16)
    scaled = (gates_in.astype(jnp.float32)[:, None] * grads_in.astype(jnp.float32)).astype(jnp.bfloat16)
    act_grad = jnp.dot(scaled, down_w, preferred_element_type=jnp.float32)
    gate_row_grad = (act_grad * pre_up * sigmoid_gate * (1.0 + pre_gate * (1.0 - sigmoid_gate))).astype(jnp.bfloat16)
    up_row_grad = (act_grad * activated).astype(jnp.bfloat16)
    input_rows = (jnp.dot(gate_row_grad, gate_w.T, preferred_element_type=jnp.float32)
                  + jnp.dot(up_row_grad, up_w.T, preferred_element_type=jnp.float32)).astype(jnp.bfloat16)
    return gate_rows, scaled, product, gate_row_grad, up_row_grad, input_rows


def rounded_sum(partial_value):
    rounded = lax.optimization_barrier(partial_value.astype(jnp.bfloat16))
    return jnp.sum(rounded.astype(jnp.float32), axis=0).astype(jnp.bfloat16)


def reference(tokens_in, out_grad, expert_ids, gate_probs, gate_up, down_proj):
    devices = N_DP * N_EXPERT
    assign = TOK_DEV * TOP_WIN
    total = TOKENS * TOP_WIN
    width = tokens_in.shape[1]
    flat_ids = expert_ids.reshape(devices, assign).astype(jnp.int32)
    onehot = (flat_ids[:, :, None] == jnp.arange(EXPERTS, dtype=jnp.int32)[None, None, :]).astype(jnp.int32)
    placed = jnp.sum((jnp.cumsum(onehot, axis=1) - onehot) * onehot, axis=2).astype(jnp.int32)
    device_ids = jnp.broadcast_to(jnp.arange(devices, dtype=jnp.int32)[:, None], (devices, assign))
    global_ids = (device_ids * assign + jnp.arange(assign, dtype=jnp.int32)[None, :]).astype(jnp.int32)
    table = jnp.full((devices, EXPERTS, CAP), total, jnp.int32).at[device_ids, flat_ids, placed].set(global_ids)
    table = table.reshape(N_DP, N_EXPERT, EXPERTS, CAP)
    tokens_pad = jnp.concatenate([tokens_in, jnp.zeros((1, width), jnp.bfloat16)], axis=0)
    grads_pad = jnp.concatenate([out_grad, jnp.zeros((1, width), jnp.bfloat16)], axis=0)
    gates_pad = jnp.concatenate([gate_probs.reshape(total), jnp.zeros((1,), jnp.bfloat16)], axis=0)
    gate_all = gate_up[:, 0]
    up_all = gate_up[:, 1]

    def per_expert(carry, expert):
        input_acc, gate_acc = carry
        picked = lax.dynamic_index_in_dim(table, expert, axis=2, keepdims=False).reshape(N_DP * N_EXPERT * CAP).astype(jnp.int32)
        token_rows = (picked // TOP_WIN).astype(jnp.int32)
        rows_in = tokens_pad[token_rows]
        grads_in = grads_pad[token_rows]
        gates_in = gates_pad[picked]
        gate_w = lax.dynamic_index_in_dim(gate_all, expert, axis=1, keepdims=False)
        up_w = lax.dynamic_index_in_dim(up_all, expert, axis=1, keepdims=False)
        down_w = lax.dynamic_index_in_dim(down_proj, expert, axis=1, keepdims=False)
        gate_rows, scaled, product, gate_row_grad, up_row_grad, input_rows = expert_rows(
            rows_in, grads_in, gates_in, gate_w, up_w, down_w)
        input_acc = input_acc.at[token_rows].add(input_rows.astype(jnp.float32))
        gate_acc = gate_acc.at[picked].set(gate_rows)
        rows_wide = rows_in.reshape(N_DP, -1, width).astype(jnp.float32)
        scaled_wide = scaled.reshape(N_DP, -1, width).astype(jnp.float32)
        gate_part = jnp.einsum('prd,prf->pdf', rows_wide, gate_row_grad.reshape(N_DP, -1, FF).astype(jnp.float32))
        up_part = jnp.einsum('prd,prf->pdf', rows_wide, up_row_grad.reshape(N_DP, -1, FF).astype(jnp.float32))
        down_part = jnp.einsum('prd,prf->pdf', scaled_wide, product.reshape(N_DP, -1, FF).astype(jnp.float32))
        return (input_acc, gate_acc), (rounded_sum(gate_part), rounded_sum(up_part), rounded_sum(down_part))

    start = (jnp.zeros((TOKENS + 1, width), jnp.float32), jnp.zeros((total + 1,), jnp.bfloat16))
    (input_acc, gate_acc), (grads_gate, grads_up, grads_down) = lax.scan(
        per_expert, start, jnp.arange(EXPERTS, dtype=jnp.int32))
    input_grad = input_acc[:TOKENS].astype(jnp.bfloat16)
    gate_grad = gate_acc[:total].reshape(TOKENS, TOP_WIN)
    gate_up_grad = jnp.stack([grads_gate, grads_up], axis=0).transpose(2, 0, 1, 3)
    down_grad = grads_down.transpose(1, 0, 2)
    return input_grad, gate_grad, gate_up_grad, down_grad
```

```python
import jax
import jax.numpy as jnp
from jax import lax
from jax.sharding import PartitionSpec as P


def body(tokens_in, out_grad, expert_ids, gate_probs, gate_up, down_proj):
    tok_dev, top_win = expert_ids.shape
    width = tokens_in.shape[1]
    n_dp = lax.axis_size("dp")
    p = lax.axis_index("dp")
    owners = lax.axis_size("expert")
    local_experts = gate_up.shape[2]
    experts = local_experts * owners
    capacity = max(2, 2 * tok_dev * top_win // experts)
    assign = tok_dev * top_win
    slots = experts * capacity
    part = width // n_dp
    f32, bf16 = jnp.float32, jnp.bfloat16

    flat_ids = expert_ids.reshape(assign)
    onehot = (flat_ids[:, None] == jnp.arange(experts, dtype=jnp.int32)[None, :]).astype(jnp.int32)
    placed = jnp.sum((jnp.cumsum(onehot, axis=0) - onehot) * onehot, axis=1)
    slot_of = flat_ids * capacity + placed
    filler = (
        jnp.full((slots,), assign, jnp.int32).at[slot_of].set(jnp.arange(assign, dtype=jnp.int32))
    )
    token_of = jnp.minimum(filler // top_win, tok_dev - 1)
    gates_pad = jnp.concatenate([gate_probs.reshape(assign), jnp.zeros((1,), bf16)], axis=0)

    def over_expert(rows):
        return lax.all_to_all(rows, "expert", split_axis=0, concat_axis=0, tiled=True)

    moved = []
    for shift in range(1, n_dp):
        perm = [(i, (i + shift) % n_dp) for i in range(n_dp)]
        to = lax.rem(p + shift, n_dp) * part
        sent = (
            lax.dynamic_slice(tokens_in, (0, to), (tok_dev, part)),
            lax.dynamic_slice(out_grad, (0, to), (tok_dev, part)),
            token_of,
        )
        moved.append(tuple(lax.ppermute(a, "dp", perm) for a in sent))

    gates_in = over_expert(gates_pad[filler].reshape(owners, local_experts, capacity))
    rows_in = over_expert(tokens_in[token_of].reshape(owners, local_experts, capacity, width))
    grads_in = over_expert(out_grad[token_of].reshape(owners, local_experts, capacity, width))
    gates_f = gates_in.astype(f32)[..., None]

    both = jnp.einsum("secd,dgef->secgf", rows_in, gate_up, preferred_element_type=f32)
    pre_gate = both[:, :, :, 0, :]
    pre_up = both[:, :, :, 1, :]
    sigmoid_gate = jax.nn.sigmoid(pre_gate)
    activated = pre_gate * sigmoid_gate
    product = activated * pre_up
    product_all = lax.all_gather((gates_f * product).astype(bf16), "dp", axis=0)

    projected = jnp.einsum("secd,def->secf", grads_in, down_proj, preferred_element_type=f32)
    gate_rows = jnp.sum(product.astype(bf16).astype(f32) * projected, axis=-1).astype(bf16)
    act_grad = gates_f * projected
    hidden = jnp.stack(
        [
            act_grad * pre_up * sigmoid_gate * (1.0 + pre_gate * (1.0 - sigmoid_gate)),
            act_grad * activated,
        ],
        axis=3,
    ).astype(bf16)
    hidden_all = lax.all_gather(hidden, "dp", axis=0)

    input_rows = jnp.einsum(
        "secgf,dgef->secd", hidden, gate_up, preferred_element_type=f32
    ).astype(bf16)
    slot_rows = over_expert(input_rows).reshape(slots, width)
    slot_gates = over_expert(gate_rows).reshape(slots)
    gate_grad = slot_gates[slot_of].reshape(tok_dev, top_win)
    places = slot_of.reshape(tok_dev, top_win)
    total = slot_rows[places[:, 0]].astype(f32)
    for k in range(1, top_win):
        total = total + slot_rows[places[:, k]].astype(f32)
    input_grad = total.astype(bf16)

    order = lax.rem(p - jnp.arange(n_dp, dtype=jnp.int32) + n_dp, n_dp)

    def columns(which, own):
        others = jnp.stack([m[which][m[2]] for m in moved])
        others = others.reshape(n_dp - 1, owners, local_experts, capacity, part)
        others = lax.all_to_all(others, "expert", split_axis=1, concat_axis=1, tiled=True)
        mine = lax.dynamic_slice_in_dim(own, p * part, part, axis=3)
        return jnp.concatenate([mine[None], others])[order]

    rows_w = columns(0, rows_in)
    grads_w = columns(1, grads_in)
    gate_up_grad = jnp.einsum(
        "psecd,psecgf->dgef", rows_w, hidden_all, preferred_element_type=f32
    ).astype(bf16)
    down_grad = jnp.einsum(
        "psecd,psecf->def", grads_w, product_all, preferred_element_type=f32
    ).astype(bf16)
    return (input_grad, gate_grad, gate_up_grad, down_grad)


def solution(mesh):
    placed = (
        P(("dp", "expert"), None),
        P(("dp", "expert"), None),
        P(("dp", "expert"), None),
        P(("dp", "expert"), None),
        P(None, None, "expert", None),
        P(None, "expert", None),
    )
    return jax.shard_map(
        body,
        mesh=mesh,
        in_specs=placed,
        out_specs=(
            P(("dp", "expert"), None),
            P(("dp", "expert"), None),
            P("dp", None, "expert", None),
            P("dp", "expert", None),
        ),
        check_vma=False,
    )
```

```python
import jax
import jax.numpy as jnp
from jax import lax
from jax.sharding import PartitionSpec as P


def body(tokens_in, out_grad, expert_ids, gate_probs, gate_up, down_proj):
    tok_dev, top_win = expert_ids.shape
    width = tokens_in.shape[1]
    n_dp = lax.axis_size("dp")
    p = lax.axis_index("dp")
    owners = lax.axis_size("expert")
    local_experts = gate_up.shape[2]
    experts = local_experts * owners
    capacity = max(2, 2 * tok_dev * top_win // experts)
    assign = tok_dev * top_win
    slots = experts * capacity
    part = width // n_dp
    f32, bf16 = jnp.float32, jnp.bfloat16

    flat_ids = expert_ids.reshape(assign)
    onehot = (flat_ids[:, None] == jnp.arange(experts, dtype=jnp.int32)[None, :]).astype(jnp.int32)
    placed = jnp.sum((jnp.cumsum(onehot, axis=0) - onehot) * onehot, axis=1)
    slot_of = flat_ids * capacity + placed
    filler = (
        jnp.full((slots,), assign, jnp.int32).at[slot_of].set(jnp.arange(assign, dtype=jnp.int32))
    )
    token_of = jnp.minimum(filler // top_win, tok_dev - 1)
    gates_pad = jnp.concatenate([gate_probs.reshape(assign), jnp.zeros((1,), bf16)], axis=0)

    def over_expert(rows):
        return lax.all_to_all(rows, "expert", split_axis=0, concat_axis=0, tiled=True)

    tokens_all = lax.all_gather(tokens_in, "expert", axis=0, tiled=True)
    out_grad_late, _ = lax.optimization_barrier((out_grad, token_of))
    grads_all = lax.all_gather(out_grad_late, "expert", axis=0, tiled=True)

    moved = []
    for shift in range(1, n_dp):
        perm = [(i, (i + shift) % n_dp) for i in range(n_dp)]
        to = lax.rem(p + shift, n_dp) * part
        cut = jnp.concatenate(
            [
                lax.dynamic_slice(tokens_in, (0, to), (tok_dev, part)),
                lax.dynamic_slice(out_grad, (0, to), (tok_dev, part)),
            ],
            axis=0,
        )
        moved.append((lax.ppermute(cut, "dp", perm), lax.ppermute(token_of, "dp", perm)))

    table = jnp.stack([token_of.astype(f32), gates_pad[filler].astype(f32)])
    table = table.reshape(2, owners, local_experts, capacity).transpose(1, 0, 2, 3)
    table = over_expert(table)
    rows_at = table[:, 0].astype(jnp.int32) + (
        jnp.arange(owners, dtype=jnp.int32)[:, None, None] * tok_dev
    )
    gates_f = table[:, 1][..., None]
    rows_in = tokens_all[rows_at.reshape(-1)].reshape(owners, local_experts, capacity, width)
    both = jnp.einsum("secd,dgef->secgf", rows_in, gate_up, preferred_element_type=f32)
    pre_gate = both[:, :, :, 0, :]
    pre_up = both[:, :, :, 1, :]
    sigmoid_gate = jax.nn.sigmoid(pre_gate)
    activated = pre_gate * sigmoid_gate
    product = activated * pre_up
    weighted = (gates_f * product).astype(bf16)
    product_all = lax.all_gather(weighted, "dp", axis=0)
    grads_all, _ = lax.optimization_barrier((grads_all, weighted))
    grads_in = grads_all[rows_at.reshape(-1)].reshape(owners, local_experts, capacity, width)

    projected = jnp.einsum("secd,def->secf", grads_in, down_proj, preferred_element_type=f32)
    gate_rows = jnp.sum(product.astype(bf16).astype(f32) * projected, axis=-1).astype(bf16)
    act_grad = gates_f * projected
    hidden = jnp.stack(
        [
            act_grad * pre_up * sigmoid_gate * (1.0 + pre_gate * (1.0 - sigmoid_gate)),
            act_grad * activated,
        ],
        axis=3,
    ).astype(bf16)
    hidden_all = lax.all_gather(hidden, "dp", axis=0)

    input_rows = jnp.einsum(
        "secgf,dgef->secd", hidden, gate_up, preferred_element_type=f32
    ).astype(bf16)
    slot_rows = over_expert(input_rows).reshape(slots, width)
    slot_gates = over_expert(gate_rows).reshape(slots)
    gate_grad = slot_gates[slot_of].reshape(tok_dev, top_win)
    places = slot_of.reshape(tok_dev, top_win)
    total = slot_rows[places[:, 0]].astype(f32)
    for k in range(1, top_win):
        total = total + slot_rows[places[:, k]].astype(f32)
    input_grad = total.astype(bf16)

    order = lax.rem(p - jnp.arange(n_dp, dtype=jnp.int32) + n_dp, n_dp)

    def columns(which, own):
        others = jnp.stack([m[0][m[1] + which * tok_dev] for m in moved])
        others = others.reshape(n_dp - 1, owners, local_experts, capacity, part)
        others, _ = lax.optimization_barrier((others, grads_all))
        others = lax.all_to_all(others, "expert", split_axis=1, concat_axis=1, tiled=True)
        mine = lax.dynamic_slice_in_dim(own, p * part, part, axis=3)
        return jnp.concatenate([mine[None], others])[order]

    rows_w = columns(0, rows_in)
    grads_w = columns(1, grads_in)
    gate_up_grad = jnp.einsum(
        "psecd,psecgf->dgef", rows_w, hidden_all, preferred_element_type=f32
    ).astype(bf16)
    down_grad = jnp.einsum(
        "psecd,psecf->def", grads_w, product_all, preferred_element_type=f32
    ).astype(bf16)
    return (input_grad, gate_grad, gate_up_grad, down_grad)


def solution(mesh):
    placed = (
        P(("dp", "expert"), None),
        P(("dp", "expert"), None),
        P(("dp", "expert"), None),
        P(("dp", "expert"), None),
        P(None, None, "expert", None),
        P(None, "expert", None),
    )
    return jax.shard_map(
        body,
        mesh=mesh,
        in_specs=placed,
        out_specs=(
            P(("dp", "expert"), None),
            P(("dp", "expert"), None),
            P("dp", None, "expert", None),
            P("dp", "expert", None),
        ),
        check_vma=False,
    )
```

```python
import jax
import jax.numpy as jnp
from jax import lax
from jax.sharding import PartitionSpec as P


def body(tokens_in, out_grad, expert_ids, gate_probs, gate_up, down_proj):
    tok_dev, top_win = expert_ids.shape
    width = tokens_in.shape[1]
    n_dp = lax.axis_size("dp")
    p = lax.axis_index("dp")
    owners = lax.axis_size("expert")
    local_experts = gate_up.shape[2]
    experts = local_experts * owners
    capacity = max(2, 2 * tok_dev * top_win // experts)
    assign = tok_dev * top_win
    slots = experts * capacity
    part = width // n_dp
    f32, bf16 = jnp.float32, jnp.bfloat16

    flat_ids = expert_ids.reshape(assign)
    onehot = (flat_ids[:, None] == jnp.arange(experts, dtype=jnp.int32)[None, :]).astype(jnp.int32)
    placed = jnp.sum((jnp.cumsum(onehot, axis=0) - onehot) * onehot, axis=1)
    slot_of = flat_ids * capacity + placed
    filler = (
        jnp.full((slots,), assign, jnp.int32).at[slot_of].set(jnp.arange(assign, dtype=jnp.int32))
    )
    token_of = jnp.minimum(filler // top_win, tok_dev - 1)
    gates_pad = jnp.concatenate([gate_probs.reshape(assign), jnp.zeros((1,), bf16)], axis=0)

    def over_expert(rows):
        return lax.all_to_all(rows, "expert", split_axis=0, concat_axis=0, tiled=True)

    rows_in = over_expert(tokens_in[token_of].reshape(owners, local_experts, capacity, width))

    moved = []
    for shift in range(1, n_dp):
        perm = [(i, (i + shift) % n_dp) for i in range(n_dp)]
        to = lax.rem(p + shift, n_dp) * part
        cut = jnp.concatenate(
            [
                lax.dynamic_slice(tokens_in, (0, to), (tok_dev, part)),
                lax.dynamic_slice(out_grad, (0, to), (tok_dev, part)),
            ],
            axis=0,
        )
        moved.append((lax.ppermute(cut, "dp", perm), lax.ppermute(token_of, "dp", perm)))

    grads_out, _ = lax.optimization_barrier(
        (out_grad[token_of].reshape(owners, local_experts, capacity, width), rows_in)
    )
    grads_in = over_expert(grads_out)
    gates_all = lax.all_gather(gates_pad[filler], "expert", axis=0)
    own = lax.axis_index("expert") * (local_experts * capacity)
    gates_in = lax.dynamic_slice(gates_all, (0, own), (owners, local_experts * capacity))
    gates_f = gates_in.reshape(owners, local_experts, capacity, 1).astype(f32)

    both = jnp.einsum("secd,dgef->secgf", rows_in, gate_up, preferred_element_type=f32)
    pre_gate = both[:, :, :, 0, :]
    pre_up = both[:, :, :, 1, :]
    sigmoid_gate = jax.nn.sigmoid(pre_gate)
    activated = pre_gate * sigmoid_gate
    product = activated * pre_up
    weighted = (gates_f * product).astype(bf16)
    product_all = lax.all_gather(weighted, "dp", axis=0)

    projected = jnp.einsum("secd,def->secf", grads_in, down_proj, preferred_element_type=f32)
    gate_rows = jnp.sum(product.astype(bf16).astype(f32) * projected, axis=-1).astype(bf16)
    act_grad = gates_f * projected
    hidden = jnp.stack(
        [
            act_grad * pre_up * sigmoid_gate * (1.0 + pre_gate * (1.0 - sigmoid_gate)),
            act_grad * activated,
        ],
        axis=3,
    ).astype(bf16)
    hidden_all = lax.all_gather(hidden, "dp", axis=0)

    input_rows = jnp.einsum(
        "secgf,dgef->secd", hidden, gate_up, preferred_element_type=f32
    ).astype(bf16)
    slot_rows = over_expert(input_rows).reshape(slots, width)
    slot_gates = over_expert(gate_rows).reshape(slots)
    gate_grad = slot_gates[slot_of].reshape(tok_dev, top_win)
    places = slot_of.reshape(tok_dev, top_win)
    total = slot_rows[places[:, 0]].astype(f32)
    for k in range(1, top_win):
        total = total + slot_rows[places[:, k]].astype(f32)
    input_grad = total.astype(bf16)

    order = lax.rem(p - jnp.arange(n_dp, dtype=jnp.int32) + n_dp, n_dp)

    def columns(which, own):
        others = jnp.stack([m[0][m[1] + which * tok_dev] for m in moved])
        others = others.reshape(n_dp - 1, owners, local_experts, capacity, part)
        others, _ = lax.optimization_barrier((others, grads_in))
        others = lax.all_to_all(others, "expert", split_axis=1, concat_axis=1, tiled=True)
        mine = lax.dynamic_slice_in_dim(own, p * part, part, axis=3)
        return jnp.concatenate([mine[None], others])[order]

    rows_w = columns(0, rows_in)
    grads_w = columns(1, grads_in)
    gate_up_grad = jnp.einsum(
        "psecd,psecgf->dgef", rows_w, hidden_all, preferred_element_type=f32
    ).astype(bf16)
    down_grad = jnp.einsum(
        "psecd,psecf->def", grads_w, product_all, preferred_element_type=f32
    ).astype(bf16)
    return (input_grad, gate_grad, gate_up_grad, down_grad)


def solution(mesh):
    placed = (
        P(("dp", "expert"), None),
        P(("dp", "expert"), None),
        P(("dp", "expert"), None),
        P(("dp", "expert"), None),
        P(None, None, "expert", None),
        P(None, "expert", None),
    )
    return jax.shard_map(
        body,
        mesh=mesh,
        in_specs=placed,
        out_specs=(
            P(("dp", "expert"), None),
            P(("dp", "expert"), None),
            P("dp", None, "expert", None),
            P("dp", "expert", None),
        ),
        check_vma=False,
    )
```

```python
import jax
import jax.numpy as jnp
from jax import lax
from jax.sharding import PartitionSpec as P


def body(tokens_in, out_grad, expert_ids, gate_probs, gate_up, down_proj):
    tok_dev, top_win = expert_ids.shape
    width = tokens_in.shape[1]
    n_dp = lax.axis_size("dp")
    p = lax.axis_index("dp")
    owners = lax.axis_size("expert")
    local_experts = gate_up.shape[2]
    experts = local_experts * owners
    capacity = max(2, 2 * tok_dev * top_win // experts)
    assign = tok_dev * top_win
    slots = experts * capacity
    part = width // n_dp
    f32, bf16 = jnp.float32, jnp.bfloat16

    flat_ids = expert_ids.reshape(assign)
    onehot = (flat_ids[:, None] == jnp.arange(experts, dtype=jnp.int32)[None, :]).astype(jnp.int32)
    placed = jnp.sum((jnp.cumsum(onehot, axis=0) - onehot) * onehot, axis=1)
    slot_of = flat_ids * capacity + placed
    filler = (
        jnp.full((slots,), assign, jnp.int32).at[slot_of].set(jnp.arange(assign, dtype=jnp.int32))
    )
    token_of = jnp.minimum(filler // top_win, tok_dev - 1)
    gates_pad = jnp.concatenate([gate_probs.reshape(assign), jnp.zeros((1,), bf16)], axis=0)

    def over_expert(rows):
        return lax.all_to_all(rows, "expert", split_axis=0, concat_axis=0, tiled=True)

    rows_in = over_expert(tokens_in[token_of].reshape(owners, local_experts, capacity, width))

    slot_table = jnp.stack([token_of.astype(f32), gates_pad[filler].astype(f32)])
    moved = []
    for shift in range(1, n_dp):
        perm = [(i, (i + shift) % n_dp) for i in range(n_dp)]
        to = lax.rem(p + shift, n_dp) * part
        cut = jnp.concatenate(
            [
                lax.dynamic_slice(tokens_in, (0, to), (tok_dev, part)),
                lax.dynamic_slice(out_grad, (0, to), (tok_dev, part)),
            ],
            axis=1,
        )
        moved.append((lax.ppermute(cut, "dp", perm), lax.ppermute(slot_table, "dp", perm)))
    rows_in, moved = lax.optimization_barrier((rows_in, moved))

    gates_out, grads_out, _ = lax.optimization_barrier(
        (
            slot_table[1].reshape(owners, local_experts, capacity),
            out_grad[token_of].reshape(owners, local_experts, capacity, width),
            rows_in,
        )
    )
    grads_in = over_expert(grads_out)
    gates_f = over_expert(gates_out)[..., None]

    both = jnp.einsum("secd,dgef->secgf", rows_in, gate_up, preferred_element_type=f32)
    pre_gate = both[:, :, :, 0, :]
    pre_up = both[:, :, :, 1, :]
    sigmoid_gate = jax.nn.sigmoid(pre_gate)
    activated = pre_gate * sigmoid_gate
    product = activated * pre_up
    product_all = lax.all_gather(product.astype(bf16), "dp", axis=0)

    projected = jnp.einsum("secd,def->secf", grads_in, down_proj, preferred_element_type=f32)
    gate_rows = jnp.sum(product.astype(bf16).astype(f32) * projected, axis=-1).astype(bf16)
    act_grad = gates_f * projected
    hidden = jnp.stack(
        [
            act_grad * pre_up * sigmoid_gate * (1.0 + pre_gate * (1.0 - sigmoid_gate)),
            act_grad * activated,
        ],
        axis=3,
    ).astype(bf16)
    hidden_all = lax.all_gather(hidden, "dp", axis=0)

    input_rows = jnp.einsum(
        "secgf,dgef->secd", hidden, gate_up, preferred_element_type=f32
    ).astype(bf16)
    slot_rows = over_expert(input_rows).reshape(slots, width)
    slot_gates = over_expert(gate_rows).reshape(slots)
    gate_grad = slot_gates[slot_of].reshape(tok_dev, top_win)
    places = slot_of.reshape(tok_dev, top_win)
    total = slot_rows[places[:, 0]].astype(f32)
    for k in range(1, top_win):
        total = total + slot_rows[places[:, k]].astype(f32)
    input_grad = total.astype(bf16)

    order = lax.rem(p - jnp.arange(n_dp, dtype=jnp.int32) + n_dp, n_dp)

    def scaled(gates, grads):
        return (gates * grads.astype(f32)).astype(bf16)

    others = []
    for cut, tab in moved:
        picked = cut[tab[0].astype(jnp.int32)]
        others.append(
            jnp.concatenate([picked[:, :part], scaled(tab[1][:, None], picked[:, part:])], axis=1)
        )
    others = jnp.stack(others).reshape(n_dp - 1, owners, local_experts, capacity, 2 * part)
    others, _ = lax.optimization_barrier((others, grads_in))
    others = lax.all_to_all(others, "expert", split_axis=1, concat_axis=1, tiled=True)
    mine = jnp.concatenate(
        [
            lax.dynamic_slice_in_dim(rows_in, p * part, part, axis=3),
            scaled(gates_f, lax.dynamic_slice_in_dim(grads_in, p * part, part, axis=3)),
        ],
        axis=3,
    )
    columns = jnp.concatenate([mine[None], others])[order]
    rows_w = columns[..., :part]
    grads_w = columns[..., part:]
    gate_up_grad = jnp.einsum(
        "psecd,psecgf->dgef", rows_w, hidden_all, preferred_element_type=f32
    ).astype(bf16)
    down_grad = jnp.einsum(
        "psecd,psecf->def", grads_w, product_all, preferred_element_type=f32
    ).astype(bf16)
    return (input_grad, gate_grad, gate_up_grad, down_grad)


def solution(mesh):
    placed = (
        P(("dp", "expert"), None),
        P(("dp", "expert"), None),
        P(("dp", "expert"), None),
        P(("dp", "expert"), None),
        P(None, None, "expert", None),
        P(None, "expert", None),
    )
    return jax.shard_map(
        body,
        mesh=mesh,
        in_specs=placed,
        out_specs=(
            P(("dp", "expert"), None),
            P(("dp", "expert"), None),
            P("dp", None, "expert", None),
            P("dp", "expert", None),
        ),
        check_vma=False,
    )
```

```python
import jax
import jax.numpy as jnp
from jax import lax
from jax.sharding import PartitionSpec as P


def body(tokens_in, out_grad, expert_ids, gate_probs, gate_up, down_proj):
    tok_dev, top_win = expert_ids.shape
    width = tokens_in.shape[1]
    n_dp = lax.axis_size("dp")
    p = lax.axis_index("dp")
    owners = lax.axis_size("expert")
    local_experts = gate_up.shape[2]
    experts = local_experts * owners
    capacity = max(2, 2 * tok_dev * top_win // experts)
    assign = tok_dev * top_win
    slots = experts * capacity
    part = width // n_dp
    f32, bf16 = jnp.float32, jnp.bfloat16

    flat_ids = expert_ids.reshape(assign)
    onehot = (flat_ids[:, None] == jnp.arange(experts, dtype=jnp.int32)[None, :]).astype(jnp.int32)
    placed = jnp.sum((jnp.cumsum(onehot, axis=0) - onehot) * onehot, axis=1)
    slot_of = flat_ids * capacity + placed
    filler = (
        jnp.full((slots,), assign, jnp.int32).at[slot_of].set(jnp.arange(assign, dtype=jnp.int32))
    )
    token_of = jnp.minimum(filler // top_win, tok_dev - 1)
    gates_pad = jnp.concatenate([gate_probs.reshape(assign), jnp.zeros((1,), bf16)], axis=0)

    def over_expert(rows):
        return lax.all_to_all(rows, "expert", split_axis=0, concat_axis=0, tiled=True)

    picks = (token_of[:, None] == jnp.arange(tok_dev, dtype=jnp.int32)[None, :]).astype(bf16)

    def to_slots(rows):
        taken = jnp.dot(picks, rows, preferred_element_type=f32).astype(bf16)
        return taken.reshape(owners, local_experts, capacity, width)

    rows_in = over_expert(to_slots(tokens_in))

    slot_gates = gates_pad[filler]
    extra = -(-2 * slots // (16 * part)) * 8
    slot_table = jnp.concatenate([token_of.astype(bf16), slot_gates])
    slot_table = jnp.pad(slot_table, (0, extra * 2 * part - 2 * slots)).reshape(extra, 2 * part)
    moved = []
    for shift in range(1, n_dp):
        perm = [(i, (i + shift) % n_dp) for i in range(n_dp)]
        to = lax.rem(p + shift, n_dp) * part
        cut = jnp.concatenate(
            [
                lax.dynamic_slice(tokens_in, (0, to), (tok_dev, part)),
                lax.dynamic_slice(out_grad, (0, to), (tok_dev, part)),
            ],
            axis=1,
        )
        moved.append(lax.ppermute(jnp.concatenate([cut, slot_table], axis=0), "dp", perm))
    rows_in, moved = lax.optimization_barrier((rows_in, moved))

    grads_out, _ = lax.optimization_barrier((to_slots(out_grad), rows_in))
    grads_in = over_expert(grads_out)
    gates_out, _ = lax.optimization_barrier((slot_gates, grads_in))
    gates_f = over_expert(gates_out.reshape(owners, local_experts, capacity))
    gates_f = gates_f[..., None].astype(f32)

    both = jnp.einsum("secd,dgef->secgf", rows_in, gate_up, preferred_element_type=f32)
    pre_gate = both[:, :, :, 0, :]
    pre_up = both[:, :, :, 1, :]
    sigmoid_gate = jax.nn.sigmoid(pre_gate)
    activated = pre_gate * sigmoid_gate
    product = activated * pre_up
    product_all = lax.all_gather(product.astype(bf16), "dp", axis=0)

    projected = jnp.einsum("secd,def->secf", grads_in, down_proj, preferred_element_type=f32)
    gate_rows = jnp.sum(product.astype(bf16).astype(f32) * projected, axis=-1).astype(bf16)
    act_grad = gates_f * projected
    hidden = jnp.stack(
        [
            act_grad * pre_up * sigmoid_gate * (1.0 + pre_gate * (1.0 - sigmoid_gate)),
            act_grad * activated,
        ],
        axis=3,
    ).astype(bf16)
    hidden_all = lax.all_gather(hidden, "dp", axis=0)

    def scaled(gates, grads):
        return (gates * grads.astype(f32)).astype(bf16)

    others = []
    for got in moved:
        tab = got[tok_dev:].reshape(-1)
        picked = got[tab[:slots].astype(jnp.int32)]
        weights = tab[slots : 2 * slots, None].astype(f32)
        others.append(
            jnp.concatenate([picked[:, :part], scaled(weights, picked[:, part:])], axis=1)
        )
    others = jnp.stack(others).reshape(n_dp - 1, owners, local_experts, capacity, 2 * part)
    others, _ = lax.optimization_barrier((others, grads_in))
    others = lax.all_to_all(others, "expert", split_axis=1, concat_axis=1, tiled=True)

    input_rows = jnp.einsum(
        "secgf,dgef->secd", hidden, gate_up, preferred_element_type=f32
    ).astype(bf16)
    input_rows, others = lax.optimization_barrier((input_rows, others))
    slot_rows = over_expert(input_rows).reshape(slots, width)
    gate_grad = over_expert(gate_rows).reshape(slots)[slot_of].reshape(tok_dev, top_win)
    places = slot_of.reshape(tok_dev, top_win)
    both_places = jnp.any(
        places[:, :, None] == jnp.arange(slots, dtype=jnp.int32)[None, None, :], axis=1
    ).astype(bf16)
    input_grad = jnp.dot(both_places, slot_rows, preferred_element_type=f32).astype(bf16)

    order = lax.rem(p - jnp.arange(n_dp, dtype=jnp.int32) + n_dp, n_dp)

    mine = jnp.concatenate(
        [
            lax.dynamic_slice_in_dim(rows_in, p * part, part, axis=3),
            scaled(gates_f, lax.dynamic_slice_in_dim(grads_in, p * part, part, axis=3)),
        ],
        axis=3,
    )
    columns = jnp.concatenate([mine[None], others])[order]
    rows_w = columns[..., :part]
    grads_w = columns[..., part:]
    gate_up_grad = jnp.einsum(
        "psecd,psecgf->dgef", rows_w, hidden_all, preferred_element_type=f32
    ).astype(bf16)
    down_grad = jnp.einsum(
        "psecd,psecf->def", grads_w, product_all, preferred_element_type=f32
    ).astype(bf16)
    return (input_grad, gate_grad, gate_up_grad, down_grad)


def solution(mesh):
    placed = (
        P(("dp", "expert"), None),
        P(("dp", "expert"), None),
        P(("dp", "expert"), None),
        P(("dp", "expert"), None),
        P(None, None, "expert", None),
        P(None, "expert", None),
    )
    return jax.shard_map(
        body,
        mesh=mesh,
        in_specs=placed,
        out_specs=(
            P(("dp", "expert"), None),
            P(("dp", "expert"), None),
            P("dp", None, "expert", None),
            P("dp", "expert", None),
        ),
        check_vma=False,
    )
```

```python
import jax
import jax.numpy as jnp
from jax import lax
from jax.sharding import PartitionSpec as P


def body(tokens_in, out_grad, expert_ids, gate_probs, gate_up, down_proj):
    tok_dev, top_win = expert_ids.shape
    width = tokens_in.shape[1]
    n_dp = lax.axis_size("dp")
    p = lax.axis_index("dp")
    owners = lax.axis_size("expert")
    local_experts = gate_up.shape[2]
    experts = local_experts * owners
    capacity = max(2, 2 * tok_dev * top_win // experts)
    assign = tok_dev * top_win
    slots = experts * capacity
    part = width // n_dp
    f32, bf16 = jnp.float32, jnp.bfloat16

    flat_ids = expert_ids.reshape(assign)
    onehot = (flat_ids[:, None] == jnp.arange(experts, dtype=jnp.int32)[None, :]).astype(jnp.int32)
    placed = jnp.sum((jnp.cumsum(onehot, axis=0) - onehot) * onehot, axis=1)
    slot_of = flat_ids * capacity + placed
    filler = (
        jnp.full((slots,), assign, jnp.int32).at[slot_of].set(jnp.arange(assign, dtype=jnp.int32))
    )
    token_of = jnp.minimum(filler // top_win, tok_dev - 1)
    gates_pad = jnp.concatenate([gate_probs.reshape(assign), jnp.zeros((1,), bf16)], axis=0)

    def over_expert(rows):
        return lax.all_to_all(rows, "expert", split_axis=0, concat_axis=0, tiled=True)

    picks = (token_of[:, None] == jnp.arange(tok_dev, dtype=jnp.int32)[None, :]).astype(bf16)

    def to_slots(rows):
        taken = jnp.dot(picks, rows, preferred_element_type=f32).astype(bf16)
        return taken.reshape(owners, local_experts, capacity, width)

    rows_in = over_expert(to_slots(tokens_in))

    slot_gates = gates_pad[filler]
    extra = -(-2 * slots // (16 * part)) * 8
    slot_table = jnp.concatenate([token_of.astype(bf16), slot_gates])
    slot_table = jnp.pad(slot_table, (0, extra * 2 * part - 2 * slots)).reshape(extra, 2 * part)
    moved = []
    for shift in range(1, n_dp):
        perm = [(i, (i + shift) % n_dp) for i in range(n_dp)]
        to = lax.rem(p + shift, n_dp) * part
        cut = jnp.concatenate(
            [
                lax.dynamic_slice(tokens_in, (0, to), (tok_dev, part)),
                lax.dynamic_slice(out_grad, (0, to), (tok_dev, part)),
            ],
            axis=1,
        )
        moved.append(lax.ppermute(jnp.concatenate([cut, slot_table], axis=0), "dp", perm))
    rows_in, moved = lax.optimization_barrier((rows_in, moved))

    grads_out, _ = lax.optimization_barrier((to_slots(out_grad), rows_in))
    grads_in = over_expert(grads_out)
    gates_out, _ = lax.optimization_barrier((slot_gates, grads_in))
    gates_f = over_expert(gates_out.reshape(owners, local_experts, capacity))
    gates_f = gates_f[..., None].astype(f32)

    both = jnp.einsum("secd,dgef->secgf", rows_in, gate_up, preferred_element_type=f32)
    pre_gate = both[:, :, :, 0, :]
    pre_up = both[:, :, :, 1, :]
    sigmoid_gate = jax.nn.sigmoid(pre_gate)
    activated = pre_gate * sigmoid_gate
    product = activated * pre_up
    product_all = lax.all_gather(product.astype(bf16), "dp", axis=0)

    projected = jnp.einsum("secd,def->secf", grads_in, down_proj, preferred_element_type=f32)
    gate_rows = jnp.sum(product.astype(bf16).astype(f32) * projected, axis=-1).astype(bf16)
    act_grad = gates_f * projected
    hidden = jnp.stack(
        [
            act_grad * pre_up * sigmoid_gate * (1.0 + pre_gate * (1.0 - sigmoid_gate)),
            act_grad * activated,
        ],
        axis=3,
    ).astype(bf16)
    hidden_all = lax.all_gather(hidden, "dp", axis=0)

    def scaled(gates, grads):
        return (gates * grads.astype(f32)).astype(bf16)

    others = []
    for got in moved:
        tab = got[tok_dev:].reshape(-1)
        picked = got[tab[:slots].astype(jnp.int32)]
        weights = tab[slots : 2 * slots, None].astype(f32)
        others.append(
            jnp.concatenate([picked[:, :part], scaled(weights, picked[:, part:])], axis=1)
        )
    others = jnp.stack(others).reshape(n_dp - 1, owners, local_experts, capacity, 2 * part)
    others, _ = lax.optimization_barrier((others, grads_in))
    others = lax.all_to_all(others, "expert", split_axis=1, concat_axis=1, tiled=True)

    input_rows = jnp.einsum(
        "secgf,dgef->secd", hidden, gate_up, preferred_element_type=f32
    ).astype(bf16)
    input_rows, others = lax.optimization_barrier((input_rows, others))
    slot_rows = over_expert(input_rows).reshape(slots, width)
    gate_rows, slot_rows = lax.optimization_barrier((gate_rows, slot_rows))
    gate_grad = over_expert(gate_rows).reshape(slots)[slot_of].reshape(tok_dev, top_win)
    places = slot_of.reshape(tok_dev, top_win)
    both_places = jnp.any(
        places[:, :, None] == jnp.arange(slots, dtype=jnp.int32)[None, None, :], axis=1
    ).astype(bf16)
    input_grad = jnp.dot(both_places, slot_rows, preferred_element_type=f32).astype(bf16)

    order = lax.rem(p - jnp.arange(n_dp, dtype=jnp.int32) + n_dp, n_dp)

    mine = jnp.concatenate(
        [
            lax.dynamic_slice_in_dim(rows_in, p * part, part, axis=3),
            scaled(gates_f, lax.dynamic_slice_in_dim(grads_in, p * part, part, axis=3)),
        ],
        axis=3,
    )
    columns = jnp.concatenate([mine[None], others])[order]
    rows_w = columns[..., :part]
    grads_w = columns[..., part:]
    gate_up_grad = jnp.einsum(
        "psecd,psecgf->dgef", rows_w, hidden_all, preferred_element_type=f32
    ).astype(bf16)
    down_grad = jnp.einsum(
        "psecd,psecf->def", grads_w, product_all, preferred_element_type=f32
    ).astype(bf16)
    return (input_grad, gate_grad, gate_up_grad, down_grad)


def solution(mesh):
    placed = (
        P(("dp", "expert"), None),
        P(("dp", "expert"), None),
        P(("dp", "expert"), None),
        P(("dp", "expert"), None),
        P(None, None, "expert", None),
        P(None, "expert", None),
    )
    return jax.shard_map(
        body,
        mesh=mesh,
        in_specs=placed,
        out_specs=(
            P(("dp", "expert"), None),
            P(("dp", "expert"), None),
            P("dp", None, "expert", None),
            P("dp", "expert", None),
        ),
        check_vma=False,
    )
```
